32 devices in a mesh: groups: 2 (over x), dp: 16 (over z, y, core).
Axes of the slice: x: 2, y: 2, z: 4, core: 2. Of those that a mesh axis runs over, the one named last changes fastest.
Arguments:
- tokens: bfloat16 [768, 8192], P(('groups', 'dp')), parts along dimension 0, may hold values from -6 to 6
- block_job: int32 [96], P('groups'), parts along dimension 0, may hold values from 0 to 15
- source: int32 [32], P('groups'), parts along dimension 0, may hold values from 0 to 47, as said below
- adapter_home: int32 [32], P('groups'), parts along dimension 0, may hold values from 0 to 15, each once
- up_weight: bfloat16 [8192, 28672], P(None, 'dp'), may hold values from -0.0625 to 0.0625
- adapter_a: bfloat16 [32, 8192, 16], P(('groups', 'dp')), parts along dimension 0, may hold values from -0.0625 to 0.0625
- adapter_b: bfloat16 [32, 16, 28672], P('groups', None, 'dp'), parts along dimension 0, may hold values from -1.5 to 1.5
- cotangent: bfloat16 [256, 28672], P('groups', 'dp'), parts along dimension 0, may hold values from -0.125 to 0.125
Outputs:
- mixed: bfloat16 [256, 28672], P('groups', 'dp'), parts along dimension 0
- grad_a: float32 [32, 8192, 16], P(('groups', 'dp')), parts along dimension 0
- grad_b: float32 [32, 16, 28672], P('groups', None, 'dp'), parts along dimension 0
The draws below stay inside these ranges and needn't reach their ends.
There are 2 independent parts, one for each index of `groups`. The reference program is written for one: setup_inputs(seed, part) draws one part's arguments, and reference() takes and returns one part's arrays. A program takes and returns all parts, laid end to end along the dimension named above; an argument that names none is the same for every part. Nothing has to cross between parts.
Inputs may be any that keep to these rules, and one draw needn't show every extreme that they name: `source`: entries are distinct block slots (device * 3 + k). The blocks a device holds before rebalancing are its slots 0 to c - 1, where c is the number of entries naming that device; c runs from 0 to 3, reaches 3 on some device, and the c sum to 16. Where c > 0, the device's own entry is its slot 0; the devices with c = 0 hold the other blocks.
All inputs are finite; a program needn't handle non-finite values.
Results may differ from the reference program's by a relative error of at most 0.0046.
Values may be sent and summed in bfloat16 or wider, within the bound.
A program may use at most 128 MiB of HBM per device.

```python
import jax
import jax.numpy as jnp

D = 8192
FF = 28672
RANK = 16
HOLD = 3
BLK = 8
JOBS = 16
ROWS = 128
N_DP = 16


count_patterns = ((3, 1, 0, 0), (2, 2, 0, 0), (2, 1, 1, 0), (1, 1, 1, 1))


def draw_source(key, part):
    key = jax.random.fold_in(key, 11)
    key_pick, key_order, key_score = jax.random.split(key, 3)
    table = jnp.array(count_patterns, jnp.int32)
    pick = jax.random.randint(key_pick, (N_DP // 4,), 0, 4)
    pick = pick.at[0].set(0)
    shuffled = table[pick].reshape(-1)
    order = jax.random.permutation(key_order, N_DP)
    counts = jnp.zeros((N_DP,), jnp.int32).at[order].set(shuffled)
    slots = jnp.arange(N_DP * HOLD, dtype=jnp.int32)
    owner = slots // HOLD
    within = slots % HOLD
    extra = (within >= 1) & (within < counts[owner])
    score = jax.random.permutation(key_score, N_DP * HOLD).astype(jnp.int32)
    extra_sorted = jnp.argsort(jnp.where(extra, score, N_DP * HOLD + score)).astype(jnp.int32)
    empty = counts == 0
    rank_empty = jnp.cumsum(empty.astype(jnp.int32)) - 1
    own_slot = jnp.arange(N_DP, dtype=jnp.int32) * HOLD
    chosen = jnp.where(empty, extra_sorted[jnp.maximum(rank_empty, 0)], own_slot)
    return chosen.astype(jnp.int32)


def set_ends(entries, own_key, least, top_value):
    extent = entries.shape
    spot = [jax.random.randint(jax.random.fold_in(own_key, axis), (), 0, extent[axis]) for axis in range(len(extent))]
    entries = entries.at[tuple(spot)].set(least)
    longest = extent.index(max(extent))
    spot[longest] = (spot[longest] + 1) % extent[longest]
    return entries.at[tuple(spot)].set(top_value)


def block_levels(key, shape, pieces, least, top_value):
    def one(dim, parts):
        steps = jax.random.uniform(jax.random.fold_in(jax.random.fold_in(key, 6), dim), (parts,), jnp.float32, least / len(pieces), top_value / len(pieces))
        return jnp.repeat(jnp.exp(steps), shape[dim] // parts).reshape((-1,) + (1,) * (len(shape) - dim - 1))

    loudness = one(*pieces[0])
    for cut in pieces[1:]:
        loudness = loudness * one(*cut)
    return loudness


def normal_values(stream_key, extent, deviation, bound, pieces=(), held_as=jnp.bfloat16):
    factor_of = block_levels(stream_key, extent, pieces, -0.22, 0.18) if pieces else 1.0
    values = jax.random.normal(stream_key, extent, jnp.float32) * deviation * factor_of
    return jnp.minimum(jnp.maximum(values, -bound), bound).astype(held_as)


def setup_inputs(seed: int = 0, part: int = 0) -> dict:
    streams_of = jax.random.split(jax.random.key(seed), 9)
    part_splits = jax.random.split(jax.random.fold_in(streams_of[8], part), 9)
    tokens = normal_values(part_splits[0], (N_DP * HOLD * BLK, D), 1.0, 6.0, ((0, 16),))
    block_job = set_ends(jax.random.randint(part_splits[1], (N_DP * HOLD,), 0, JOBS), jax.random.fold_in(part_splits[1], 1), 0, JOBS - 1).astype(jnp.int32)
    source = draw_source(jax.random.fold_in(jax.random.fold_in(streams_of[8], part), 71), part)
    adapter_home = jax.random.permutation(part_splits[3], JOBS).astype(jnp.int32)
    up_weight = normal_values(streams_of[4], (D, FF), D ** -0.5, 0.0625, ((1, 16),))
    adapter_a = normal_values(part_splits[5], (JOBS, D, RANK), D ** -0.5, 0.0625, ((0, 16),))
    adapter_b = normal_values(part_splits[6], (JOBS, RANK, FF), RANK ** -0.5, 1.5, ((2, 16),))
    cotangent = normal_values(part_splits[7], (ROWS, FF), 0.02, 0.125, ((1, 16),))
    return dict(tokens=tokens, block_job=block_job, source=source, adapter_home=adapter_home, up_weight=up_weight, adapter_a=adapter_a, adapter_b=adapter_b, cotangent=cotangent)


SCALE = 2.0


def reference(tokens, block_job, source, adapter_home, up_weight, adapter_a, adapter_b, cotangent):
    picked = tokens.reshape(N_DP * HOLD, BLK, D)[source]
    slot = adapter_home[block_job[source]].astype(jnp.int32)
    base_out = jnp.dot(picked.reshape(-1, D), up_weight, preferred_element_type=jnp.float32)
    factor_a = adapter_a[slot]
    code_sum = jnp.einsum("nbd,ndr->nbr", picked.astype(jnp.float32), factor_a.astype(jnp.float32))
    codes_b = code_sum.astype(jnp.bfloat16)
    factor_b = adapter_b[slot]
    low_rank = jnp.einsum("nbr,nrf->nbf", codes_b.astype(jnp.float32), factor_b.astype(jnp.float32))
    mixed = (base_out + SCALE * low_rank.reshape(-1, FF)).astype(jnp.bfloat16)
    upstream = cotangent.reshape(N_DP, BLK, FF).astype(jnp.float32)
    back_sum = jnp.einsum("nbf,nrf->nbr", upstream, factor_b.astype(jnp.float32))
    back_b = back_sum.astype(jnp.bfloat16)
    per_block_b = jnp.einsum("nbr,nbf->nrf", codes_b.astype(jnp.float32), upstream)
    grad_b = SCALE * jnp.zeros((JOBS, RANK, FF), jnp.float32).at[slot].add(per_block_b)
    per_block_a = jnp.einsum("nbd,nbr->ndr", picked.astype(jnp.float32), back_b.astype(jnp.float32))
    grad_a = SCALE * jnp.zeros((JOBS, D, RANK), jnp.float32).at[slot].add(per_block_a)
    return mixed, grad_a, grad_b
```

```python
import functools

import jax
import jax.numpy as jnp
from jax import lax
from jax.experimental import pallas as pl
from jax.experimental.pallas import tpu as pltpu
from jax.sharding import PartitionSpec as P

HOLD = 3
SCALE = 2.0
W_PARTS = 8


def dot(a, b, dims=((1,), (0,))):
    return lax.dot_general(a, b, (dims, ((), ())), preferred_element_type=jnp.float32)


def kernel(n, rows_y, rank, source, block_job, adapter_home, tokens, up_weight, adapter_a, adapter_b,
           cotangent, mixed, grad_a, grad_b, weight, factor_a, factor_b, upstream, stage, picked, total, code_acc,
           back_out, back_in, codes, load_sem, stage_send, stage_recv, back_send, back_recv, code_send,
           code_recv, ring_send, ring_recv, pair_send, pair_recv):
    rows, width = cotangent.shape[0], tokens.shape[1]
    blk = rows // n
    chunk = width // n
    chips = n // 2
    half = chips // 2
    length = chips // rows_y
    me = lax.axis_index("dp")
    core = me % 2
    chip = me // 2
    line, depth = chip % rows_y, chip // rows_y
    place = depth + line * (chips - 1 - 2 * depth)
    step = 1 - 2 * core
    sibling = chip * 2 + 1 - core

    def chip_at(position):
        position = (position + 2 * chips) % chips
        turn, along = position // length, position % length
        return (along + turn * (length - 1 - 2 * along)) * rows_y + turn

    following = chip_at(place + step) * 2 + core

    def local(src, dst, index):
        return pltpu.make_async_copy(src, dst, load_sem.at[index])

    def remote(src, dst, sent, got, target):
        return pltpu.make_async_remote_copy(src, dst, sent, got, device_id={"dp": target},
                                            device_id_type=pl.DeviceIdType.MESH)

    barrier = pltpu.get_barrier_semaphore()

    def greet(offset, carry):
        pl.semaphore_signal(barrier, inc=1, device_id={"dp": (me + offset) % n}, device_id_type=pl.DeviceIdType.MESH)
        return carry

    lax.fori_loop(1, n, greet, 0)

    def columns(k):
        return pl.ds(pl.multiple_of(k * chunk, chunk), chunk)

    own = local(tokens.at[:, columns(me)], stage.at[me], 0)
    load_up = local(cotangent, upstream, 1)
    load_b = local(adapter_b, factor_b, 2)
    load_a = local(adapter_a, factor_a, 3)
    share = width // W_PARTS
    load_w = [local(up_weight.at[pl.ds(i * share, share)], weight.at[pl.ds(i * share, share)], 4 + i)
              for i in range(W_PARTS)]
    for copy in (own, load_up, load_b, load_a):
        copy.start()
    pl.semaphore_wait(barrier, n - 1)

    def stage_copy(offset):
        k = (me + offset) % n
        return remote(tokens.at[:, columns(k)], stage.at[me], stage_send.at[offset], stage_recv.at[offset], k)

    def each(body):
        def run(offset, carry):
            body(offset)
            return carry
        lax.fori_loop(1, n, run, 0)

    each(lambda offset: stage_copy(offset).start())
    for copy in load_w:
        copy.start()

    load_up.wait()
    load_b.wait()
    back_out[...] = dot(factor_b[...], upstream[...], ((1,), (1,))).reshape(n, rank, rows)
    back_in[me] = back_out[me]

    def back_copy(offset):
        k = (me + offset) % n
        return remote(back_out.at[k], back_in.at[me], back_send.at[offset], back_recv.at[offset], k)

    lane = lax.broadcasted_iota(jnp.int32, (8, rows), 1) // blk
    slot_of = jnp.zeros((8, rows), jnp.int32)
    row_block = lax.broadcasted_iota(jnp.int32, (rows, 128), 0) // blk
    source_of = jnp.zeros((rows, 128), jnp.int32)
    for e in range(n):
        origin = source[e]
        home = adapter_home[block_job[origin]]
        slot_of = jnp.where(lane == e, home, slot_of)
        source_of = jnp.where(row_block == e, origin, source_of)
    places = n * HOLD * blk
    at = lax.broadcasted_iota(jnp.int32, (rows, places), 1)
    row = lax.broadcasted_iota(jnp.int32, (rows, places), 0)
    wanted = source_of[:, :1] * blk + row % blk
    choose = jnp.where(at == wanted, 1.0, 0.0).astype(jnp.bfloat16)

    own.wait()
    each(lambda offset: stage_copy(offset).wait_recv())
    held = stage[...].astype(jnp.float32).reshape(places, chunk).astype(jnp.bfloat16)
    picked[me] = dot(choose, held).astype(jnp.bfloat16)

    def piece(t, h, away=-1):
        return chip_at(place + away * t * step) * 2 + (core + h) % 2

    def ring(t, h):
        k = piece(t, h)
        return remote(picked.at[k], picked.at[k], ring_send.at[2 * t + h], ring_recv.at[2 * t + h], following)

    def pair(t, h):
        k = piece(t, h)
        return remote(picked.at[k], picked.at[k], pair_send.at[2 * t + h], pair_recv.at[2 * t + h], sibling)

    def use(k):
        part = picked[k]
        total[...] += dot(part, weight[columns(k), :])
        code_acc[...] += dot(factor_a[:, columns(k)], part, ((1,), (1,)))

    pair(0, 0).start()
    ring(0, 0).start()
    each(lambda offset: back_copy(offset).start())
    total[...] = jnp.zeros_like(total)
    code_acc[...] = jnp.zeros_like(code_acc)
    pair(0, 0).wait_recv()
    ring(0, 1).start()
    load_a.wait()
    for copy in load_w:
        copy.wait()
    use(me)
    use(sibling)

    def hop(t, carry):
        for h in range(2):
            ring(t - 1, h).wait_recv()
            pair(t, h).start()
            if h == 0:
                ring(t, 0).start()
            else:
                @pl.when(t < half - 1)
                def _():
                    ring(t, 1).start()
            use(piece(t, h))
        for h in range(2):
            pair(t, h).wait_recv()
            use(piece(t, 1 - h, 1))
        return carry

    lax.fori_loop(1, half, hop, 0)
    ring(half - 1, 0).wait_recv()
    pair(half, 0).start()
    use(piece(half, 0))
    pair(half, 0).wait_recv()
    use(piece(half, 1, 1))

    codes[me] = code_acc[...].astype(jnp.bfloat16)

    def code_copy(offset):
        k = (me + offset) % n
        return remote(codes.at[me], codes.at[me], code_send.at[offset], code_recv.at[offset], k)

    each(lambda offset: code_copy(offset).start())

    each(lambda offset: back_copy(offset).wait_recv())
    back_sum = jnp.sum(back_in[...], axis=0)
    back_b = jnp.where(slot_of[:1] == me, back_sum, 0.0).astype(jnp.bfloat16)
    for k in range(n):
        grad_a[:, k * chunk:(k + 1) * chunk] = SCALE * dot(back_b, picked[k])

    each(lambda offset: code_copy(offset).wait_recv())
    adapter_of = lax.broadcasted_iota(jnp.int32, (n * rank, rows), 0) // rank
    code_rows = codes[...].astype(jnp.float32).reshape(n * rank, rows)
    code_rows = jnp.where(slot_of[:1] == adapter_of, code_rows, 0.0)
    code_b = code_rows.astype(jnp.bfloat16)
    mixed[...] = (total[...] + SCALE * dot(code_rows.T.astype(jnp.bfloat16), factor_b[...])).astype(jnp.bfloat16)
    grad_b[...] = SCALE * dot(code_b, upstream[...])

    each(lambda offset: stage_copy(offset).wait_send())
    each(lambda offset: back_copy(offset).wait_send())
    each(lambda offset: code_copy(offset).wait_send())

    def ended(t, carry):
        ring(t, 0).wait_send()
        pair(t, 0).wait_send()
        return carry

    def ended_other(t, carry):
        ring(t - 1, 1).wait_send()
        pair(t, 1).wait_send()
        return carry

    lax.fori_loop(0, half, ended, 0)
    pair(half, 0).wait_send()
    lax.fori_loop(1, half, ended_other, 0)


def on_device(rows_y, tokens, block_job, source, adapter_home, up_weight, adapter_a, adapter_b, cotangent):
    n = lax.axis_size("dp")
    width = tokens.shape[1]
    rows, hidden = cotangent.shape
    jobs, rank, _ = adapter_b.shape
    chunk = width // n
    smem = pl.BlockSpec(memory_space=pltpu.SMEM)
    anywhere = pl.BlockSpec(memory_space=pl.ANY)
    vmem = pl.BlockSpec(memory_space=pltpu.VMEM)
    bf16, f32 = jnp.bfloat16, jnp.float32
    dma = lambda count: pltpu.SemaphoreType.DMA((count,))
    mixed, grad_a, grad_b = pl.pallas_call(
        functools.partial(kernel, n, rows_y, rank),
        out_shape=(
            jax.ShapeDtypeStruct((rows, hidden), bf16),
            jax.ShapeDtypeStruct((rank, width), f32),
            jax.ShapeDtypeStruct((jobs * rank, hidden), f32),
        ),
        in_specs=[smem] * 3 + [anywhere] * 5,
        out_specs=(vmem,) * 3,
        scratch_shapes=[
            pltpu.VMEM((width, hidden), bf16),
            pltpu.VMEM((rank, width), bf16),
            pltpu.VMEM((jobs * rank, hidden), bf16),
            pltpu.VMEM((rows, hidden), bf16),
            pltpu.VMEM((n,) + (tokens.shape[0], chunk), bf16),
            pltpu.VMEM((n, rows, chunk), bf16),
            pltpu.VMEM((rows, hidden), f32),
            pltpu.VMEM((rank, rows), f32),
            pltpu.VMEM((n, rank, rows), f32),
            pltpu.VMEM((n, rank, rows), f32),
            pltpu.VMEM((n, rank, rows), bf16),
            dma(4 + W_PARTS),
        ] + [dma(n)] * 6 + [dma(n)] * 2 + [dma(n + 2)] * 2,
        compiler_params=pltpu.CompilerParams(
            collective_id=0, has_side_effects=True, vmem_limit_bytes=56 * 1024 * 1024
        ),
    )(
        source, block_job, adapter_home, tokens, up_weight, adapter_a[0].T,
        adapter_b.reshape(jobs * rank, hidden), cotangent,
    )
    return mixed, grad_a.T[None], grad_b.reshape(jobs, rank, hidden)


def solution(mesh):
    placed = (
        P(("groups", "dp"), None),
        P("groups"),
        P("groups"),
        P("groups"),
        P(None, "dp"),
        P(("groups", "dp"), None, None),
        P("groups", None, "dp"),
        P("groups", "dp"),
    )
    rows_y = 2 if mesh.shape["groups"] == 2 else 1
    return jax.shard_map(
        functools.partial(on_device, rows_y),
        mesh=mesh,
        in_specs=placed,
        out_specs=(P("groups", "dp"), P(("groups", "dp"), None, None), P("groups", None, "dp")),
        check_vma=False,
    )
```

```python
import functools

import jax
import jax.numpy as jnp
from jax import lax
from jax.experimental import pallas as pl
from jax.experimental.pallas import tpu as pltpu
from jax.sharding import PartitionSpec as P

HOLD = 3
SCALE = 2.0
W_PARTS = 8
SPLIT = 2
OUT_PARTS = 4


def dot(a, b, dims=((1,), (0,))):
    return lax.dot_general(a, b, (dims, ((), ())), preferred_element_type=jnp.float32)


def kernel(n, rows_y, rank, source, block_job, adapter_home, tokens, up_weight, adapter_a, adapter_b,
           cotangent, total_out, grad_a_out, codes_out, weight, factor_a, factor_b, upstream, stage, picked, total, code_acc,
           grad_a, code_b, back_out, back_pair, back_in, codes, load_sem, stage_send, stage_recv, back_send, back_recv,
           code_send, code_recv, ring_send, ring_recv, pair_send, pair_recv):
    rows, width = cotangent.shape[0], tokens.shape[1]
    blk = rows // n
    chunk = width // n
    chips = n // 2
    half = chips // 2
    length = chips // rows_y
    me = lax.axis_index("dp")
    core = me % 2
    chip = me // 2
    line, depth = chip % rows_y, chip // rows_y
    place = depth + line * (chips - 1 - 2 * depth)
    step = 1 - 2 * core
    sibling = chip * 2 + 1 - core

    def chip_at(position):
        position = (position + 2 * chips) % chips
        turn, along = position // length, position % length
        return (along + turn * (length - 1 - 2 * along)) * rows_y + turn

    following = chip_at(place + step) * 2 + core

    def local(src, dst, index):
        return pltpu.make_async_copy(src, dst, load_sem.at[index])

    def remote(src, dst, sent, got, target):
        return pltpu.make_async_remote_copy(src, dst, sent, got, device_id={"dp": target},
                                            device_id_type=pl.DeviceIdType.MESH)

    barrier = pltpu.get_barrier_semaphore()

    def greet(offset, carry):
        pl.semaphore_signal(barrier, inc=1, device_id={"dp": (me + offset) % n}, device_id_type=pl.DeviceIdType.MESH)
        return carry

    lax.fori_loop(1, n, greet, 0)

    def columns(k):
        return pl.ds(pl.multiple_of(k * chunk, chunk), chunk)

    own = local(tokens.at[:, columns(me)], stage.at[me], 0)
    load_up = local(cotangent, upstream, 1)
    load_b = local(adapter_b, factor_b, 2)
    load_a = local(adapter_a, factor_a, 3)
    share = width // W_PARTS
    load_w = [local(up_weight.at[pl.ds(i * share, share)], weight.at[pl.ds(i * share, share)], 4 + i)
              for i in range(W_PARTS)]
    for copy in [own, load_up, load_b, load_a] + load_w:
        copy.start()
    pl.semaphore_wait(barrier, n - 1)

    def stage_copy(offset):
        k = (me + offset) % n
        return remote(tokens.at[:, columns(k)], stage.at[me], stage_send.at[offset], stage_recv.at[offset], k)

    def each(body):
        def run(offset, carry):
            body(offset)
            return carry
        lax.fori_loop(1, n, run, 0)

    each(lambda offset: stage_copy(offset).start())

    load_up.wait()
    load_b.wait()
    back_out[...] = dot(factor_b[...], upstream[...], ((1,), (1,))).reshape(chips, 2, rank, rows)
    back_half = remote(back_out.at[:, 1 - core], back_pair, back_send.at[0], back_recv.at[0], sibling)
    back_half.start()

    def back_copy(offset):
        to = (chip + offset) % chips
        return remote(back_out.at[to, core], back_in.at[chip], back_send.at[offset], back_recv.at[offset], to * 2 + core)

    def each_chip(body):
        def run(offset, carry):
            body(offset)
            return carry
        lax.fori_loop(1, chips, run, 0)

    lane = lax.broadcasted_iota(jnp.int32, (8, rows), 1) // blk
    slot_of = jnp.zeros((8, rows), jnp.int32)
    row_block = lax.broadcasted_iota(jnp.int32, (rows, 128), 0) // blk
    source_of = jnp.zeros((rows, 128), jnp.int32)
    for e in range(n):
        origin = source[e]
        home = adapter_home[block_job[origin]]
        slot_of = jnp.where(lane == e, home, slot_of)
        source_of = jnp.where(row_block == e, origin, source_of)
    places = n * HOLD * blk
    at = lax.broadcasted_iota(jnp.int32, (rows, places), 1)
    row = lax.broadcasted_iota(jnp.int32, (rows, places), 0)
    wanted = source_of[:, :1] * blk + row % blk
    choose = jnp.where(at == wanted, 1.0, 0.0).astype(jnp.bfloat16)

    own.wait()
    each(lambda offset: stage_copy(offset).wait_recv())
    held = stage[...].astype(jnp.float32).reshape(places, chunk).astype(jnp.bfloat16)
    picked[me] = dot(choose, held).astype(jnp.bfloat16)

    def piece(t, h, away=-1):
        return chip_at(place + away * t * step) * 2 + (core + h) % 2

    cut = rows // SPLIT

    def ring(t, h, i):
        k = piece(t, h)
        at, index = pl.ds(i * cut, cut), (2 * t + h) * SPLIT + i
        return remote(picked.at[k, at], picked.at[k, at], ring_send.at[index], ring_recv.at[index], following)

    def pair(t, h, i):
        k = piece(t, h)
        at, index = pl.ds(i * cut, cut), (2 * t + h) * SPLIT + i
        return remote(picked.at[k, at], picked.at[k, at], pair_send.at[index], pair_recv.at[index], sibling)

    def use(k):
        part = picked[k]
        total[...] += dot(part, weight[columns(k), :])
        code_acc[...] += dot(factor_a[:, columns(k)], part, ((1,), (1,)))

    for i in range(SPLIT):
        pair(0, 0, i).start()
        ring(0, 0, i).start()
    total[...] = jnp.zeros_like(total)
    code_acc[...] = jnp.zeros_like(code_acc)
    for i in range(SPLIT):
        pair(0, 0, i).wait_recv()
        ring(0, 1, i).start()
    back_half.wait()
    for c in range(chips):
        back_out[c, core] = back_out[c, core] + back_pair[c]
    back_in[chip] = back_out[chip, core]
    each_chip(lambda offset: back_copy(offset).start())
    load_a.wait()
    for copy in load_w:
        copy.wait()
    use(me)

    def forward(t, h):
        for i in range(SPLIT):
            ring(t - 1, h, i).wait_recv()
            pair(t, h, i).start()
            if h == 0:
                ring(t, 0, i).start()
            else:
                @pl.when(t < half - 1)
                def _():
                    ring(t, 1, i).start()

    def hop(t, carry):
        forward(t, 0)
        use(jnp.where(t == 1, sibling, piece(t - 1, 1)))
        forward(t, 1)
        use(piece(t, 0))

        @pl.when(t > 1)
        def _():
            for h in range(2):
                for i in range(SPLIT):
                    pair(t - 1, h, i).wait_recv()
                use(piece(t - 1, 1 - h, 1))
        return carry

    lax.fori_loop(1, half, hop, 0)
    for i in range(SPLIT):
        ring(half - 1, 0, i).wait_recv()
        pair(half, 0, i).start()
    use(sibling if half == 1 else piece(half - 1, 1))
    use(piece(half, 0))
    if half > 1:
        for h in range(2):
            for i in range(SPLIT):
                pair(half - 1, h, i).wait_recv()
            use(piece(half - 1, 1 - h, 1))
    for i in range(SPLIT):
        pair(half, 0, i).wait_recv()
    use(piece(half, 1, 1))

    codes[me] = code_acc[...].astype(jnp.bfloat16)

    def code_copy(offset):
        k = (me + offset) % n
        return remote(codes.at[me], codes.at[me], code_send.at[offset], code_recv.at[offset], k)

    each(lambda offset: code_copy(offset).start())

    store_total = local(total, total_out, 0)
    store_total.start()
    each_chip(lambda offset: back_copy(offset).wait_recv())
    back_sum = jnp.sum(back_in[...], axis=0)
    back_b = jnp.where(slot_of[:1] == me, back_sum, 0.0).astype(jnp.bfloat16)
    for k in range(n):
        grad_a[:, k * chunk:(k + 1) * chunk] = SCALE * dot(back_b, picked[k])
    store_a = local(grad_a, grad_a_out, 1)
    store_a.start()

    adapter_of = lax.broadcasted_iota(jnp.int32, (n * rank, rows), 0) // rank
    each(lambda offset: code_copy(offset).wait_recv())
    code_rows = codes[...].astype(jnp.float32).reshape(n * rank, rows)
    code_b[...] = jnp.where(slot_of[:1] == adapter_of, code_rows, 0.0).astype(jnp.bfloat16)
    store_codes = local(code_b, codes_out, 2)
    store_codes.start()

    each(lambda offset: stage_copy(offset).wait_send())
    each(lambda offset: code_copy(offset).wait_send())
    each_chip(lambda offset: back_copy(offset).wait_send())

    def ended(t, carry):
        for i in range(SPLIT):
            ring(t, 0, i).wait_send()
            pair(t, 0, i).wait_send()
        return carry

    def ended_other(t, carry):
        for i in range(SPLIT):
            ring(t - 1, 1, i).wait_send()
            pair(t, 1, i).wait_send()
        return carry

    lax.fori_loop(0, half, ended, 0)
    for i in range(SPLIT):
        pair(half, 0, i).wait_send()
    lax.fori_loop(1, half, ended_other, 0)
    for copy in (store_total, store_a, store_codes):
        copy.wait()


def finish(total_in, grad_a_in, codes_in, adapter_b, cotangent, mixed_out, grad_a_out, grad_b_out, total, codes,
           factor_b, upstream, grad_a, mixed, grad_b, sem):
    def local(src, dst, index):
        return pltpu.make_async_copy(src, dst, sem.at[index])

    loads = [local(codes_in, codes, 0), local(cotangent, upstream, 1), local(adapter_b, factor_b, 2),
             local(total_in, total, 3), local(grad_a_in, grad_a, 4)]
    for copy in loads:
        copy.start()
    stores = []
    loads[0].wait()
    loads[1].wait()
    share = grad_b.shape[0] // OUT_PARTS
    for i in range(OUT_PARTS):
        at = pl.ds(i * share, share)
        grad_b[at] = SCALE * dot(codes[at], upstream[...])
        stores.append(local(grad_b.at[at], grad_b_out.at[at], 7 + i))
        stores[-1].start()
    loads[4].wait()
    stores.append(local(grad_a, grad_a_out, 5))
    stores[-1].start()
    loads[2].wait()
    loads[3].wait()
    code_rows = codes[...].astype(jnp.float32).T.astype(jnp.bfloat16)
    mixed[...] = (total[...] + SCALE * dot(code_rows, factor_b[...])).astype(jnp.bfloat16)
    stores.append(local(mixed, mixed_out, 6))
    stores[-1].start()
    for copy in stores:
        copy.wait()


def on_device(rows_y, tokens, block_job, source, adapter_home, up_weight, adapter_a, adapter_b, cotangent):
    n = lax.axis_size("dp")
    width = tokens.shape[1]
    rows, hidden = cotangent.shape
    jobs, rank, _ = adapter_b.shape
    chunk = width // n
    factor_b = adapter_b.reshape(jobs * rank, hidden)
    smem = pl.BlockSpec(memory_space=pltpu.SMEM)
    anywhere = pl.BlockSpec(memory_space=pl.ANY)
    bf16, f32 = jnp.bfloat16, jnp.float32
    dma = lambda count: pltpu.SemaphoreType.DMA((count,))
    base, grad_a, codes = pl.pallas_call(
        functools.partial(kernel, n, rows_y, rank),
        out_shape=(
            jax.ShapeDtypeStruct((rows, hidden), f32),
            jax.ShapeDtypeStruct((rank, width), f32),
            jax.ShapeDtypeStruct((jobs * rank, rows), bf16),
        ),
        in_specs=[smem] * 3 + [anywhere] * 5,
        out_specs=(anywhere,) * 3,
        scratch_shapes=[
            pltpu.VMEM((width, hidden), bf16),
            pltpu.VMEM((rank, width), bf16),
            pltpu.VMEM((jobs * rank, hidden), bf16),
            pltpu.VMEM((rows, hidden), bf16),
            pltpu.VMEM((n,) + (tokens.shape[0], chunk), bf16),
            pltpu.VMEM((n, rows, chunk), bf16),
            pltpu.VMEM((rows, hidden), f32),
            pltpu.VMEM((rank, rows), f32),
            pltpu.VMEM((rank, width), f32),
            pltpu.VMEM((jobs * rank, rows), bf16),
            pltpu.VMEM((n // 2, 2, rank, rows), f32),
            pltpu.VMEM((n // 2, rank, rows), f32),
            pltpu.VMEM((n // 2, rank, rows), f32),
            pltpu.VMEM((n, rank, rows), bf16),
            dma(4 + W_PARTS),
        ] + [dma(n)] * 2 + [dma(n // 2)] * 2 + [dma(n)] * 2 + [dma(n * SPLIT)] * 2 + [dma((n // 2 + 1) * SPLIT)] * 2,
        compiler_params=pltpu.CompilerParams(
            collective_id=0, has_side_effects=True, vmem_limit_bytes=60 * 1024 * 1024
        ),
    )(
        source, block_job, adapter_home, tokens, up_weight, adapter_a[0].T,
        factor_b, cotangent,
    )
    mixed, grad_a, grad_b = pl.pallas_call(
        finish,
        out_shape=(
            jax.ShapeDtypeStruct((rows, hidden), bf16),
            jax.ShapeDtypeStruct((rank, width), f32),
            jax.ShapeDtypeStruct((jobs * rank, hidden), f32),
        ),
        in_specs=[anywhere] * 5,
        out_specs=(anywhere,) * 3,
        scratch_shapes=[
            pltpu.VMEM((rows, hidden), f32),
            pltpu.VMEM((jobs * rank, rows), bf16),
            pltpu.VMEM((jobs * rank, hidden), bf16),
            pltpu.VMEM((rows, hidden), bf16),
            pltpu.VMEM((rank, width), f32),
            pltpu.VMEM((rows, hidden), bf16),
            pltpu.VMEM((jobs * rank, hidden), f32),
            dma(7 + OUT_PARTS),
        ],
        compiler_params=pltpu.CompilerParams(vmem_limit_bytes=60 * 1024 * 1024),
    )(base, grad_a, codes, factor_b, cotangent)
    return mixed, grad_a.T[None], grad_b.reshape(jobs, rank, hidden)


def solution(mesh):
    placed = (
        P(("groups", "dp"), None),
        P("groups"),
        P("groups"),
        P("groups"),
        P(None, "dp"),
        P(("groups", "dp"), None, None),
        P("groups", None, "dp"),
        P("groups", "dp"),
    )
    rows_y = 2 if mesh.shape["groups"] == 2 else 1
    return jax.shard_map(
        functools.partial(on_device, rows_y),
        mesh=mesh,
        in_specs=placed,
        out_specs=(P("groups", "dp"), P(("groups", "dp"), None, None), P("groups", None, "dp")),
        check_vma=False,
    )
```

```python
import functools

import jax
import jax.numpy as jnp
from jax import lax
from jax.experimental import pallas as pl
from jax.experimental.pallas import tpu as pltpu
from jax.sharding import PartitionSpec as P

HOLD = 3
SCALE = 2.0
W_PARTS = 8
SPLIT = 2
OUT_PARTS = 4


def dot(a, b, dims=((1,), (0,))):
    return lax.dot_general(a, b, (dims, ((), ())), preferred_element_type=jnp.float32)


def kernel(n, rows_y, rank, source, block_job, adapter_home, tokens, up_weight, adapter_a, adapter_b,
           cotangent, total_out, grad_a_out, codes_out, weight, factor_a, factor_b, upstream, stage, picked, total, code_acc,
           grad_a, code_b, back_out, back_pair, back_in, codes, load_sem, stage_send, stage_recv, back_send, back_recv,
           code_send, code_recv, ring_send, ring_recv, pair_send, pair_recv):
    rows, width = cotangent.shape[0], tokens.shape[1]
    blk = rows // n
    chunk = width // n
    chips = n // 2
    half = chips // 2
    length = chips // rows_y
    me = lax.axis_index("dp")
    core = me % 2
    chip = me // 2
    line, depth = chip % rows_y, chip // rows_y
    place = depth + line * (chips - 1 - 2 * depth)
    step = 1 - 2 * core
    sibling = chip * 2 + 1 - core

    def chip_at(position):
        position = (position + 2 * chips) % chips
        turn, along = position // length, position % length
        return (along + turn * (length - 1 - 2 * along)) * rows_y + turn

    following = chip_at(place + step) * 2 + core

    def local(src, dst, index):
        return pltpu.make_async_copy(src, dst, load_sem.at[index])

    def remote(src, dst, sent, got, target):
        return pltpu.make_async_remote_copy(src, dst, sent, got, device_id={"dp": target},
                                            device_id_type=pl.DeviceIdType.MESH)

    barrier = pltpu.get_barrier_semaphore()

    def greet(offset, carry):
        pl.semaphore_signal(barrier, inc=1, device_id={"dp": (me + offset) % n}, device_id_type=pl.DeviceIdType.MESH)
        return carry

    lax.fori_loop(1, n, greet, 0)

    def columns(k):
        return pl.ds(pl.multiple_of(k * chunk, chunk), chunk)

    own = local(tokens.at[:, columns(me)], stage.at[me], 0)
    load_up = local(cotangent, upstream, 1)
    load_b = local(adapter_b, factor_b, 2)
    load_a = local(adapter_a, factor_a, 3)
    share = width // W_PARTS
    load_w = [local(up_weight.at[pl.ds(i * share, share)], weight.at[pl.ds(i * share, share)], 4 + i)
              for i in range(W_PARTS)]
    for copy in [own, load_up, load_b, load_a] + load_w:
        copy.start()
    pl.semaphore_wait(barrier, n - 1)

    def stage_copy(offset):
        k = (me + offset) % n
        return remote(tokens.at[:, columns(k)], stage.at[me], stage_send.at[offset], stage_recv.at[offset], k)

    def each(body):
        def run(offset, carry):
            body(offset)
            return carry
        lax.fori_loop(1, n, run, 0)

    each(lambda offset: stage_copy(offset).start())

    load_up.wait()
    load_b.wait()
    back_out[...] = dot(factor_b[...], upstream[...], ((1,), (1,))).reshape(chips, 2, rank, rows)
    back_half = remote(back_out.at[:, 1 - core], back_pair, back_send.at[0], back_recv.at[0], sibling)
    back_half.start()

    def back_copy(offset):
        to = (chip + offset) % chips
        return remote(back_out.at[to, core], back_in.at[chip], back_send.at[offset], back_recv.at[offset], to * 2 + core)

    def each_chip(body):
        def run(offset, carry):
            body(offset)
            return carry
        lax.fori_loop(1, chips, run, 0)

    lane = lax.broadcasted_iota(jnp.int32, (8, rows), 1) // blk
    slot_of = jnp.zeros((8, rows), jnp.int32)
    row_block = lax.broadcasted_iota(jnp.int32, (rows, 128), 0) // blk
    source_of = jnp.zeros((rows, 128), jnp.int32)
    for e in range(n):
        origin = source[e]
        home = adapter_home[block_job[origin]]
        slot_of = jnp.where(lane == e, home, slot_of)
        source_of = jnp.where(row_block == e, origin, source_of)
    places = n * HOLD * blk
    at = lax.broadcasted_iota(jnp.int32, (rows, places), 1)
    row = lax.broadcasted_iota(jnp.int32, (rows, places), 0)
    wanted = source_of[:, :1] * blk + row % blk
    choose = jnp.where(at == wanted, 1.0, 0.0).astype(jnp.bfloat16)

    own.wait()
    each(lambda offset: stage_copy(offset).wait_recv())
    held = stage[...].astype(jnp.float32).reshape(places, chunk).astype(jnp.bfloat16)
    picked[me] = dot(choose, held).astype(jnp.bfloat16)

    def piece(t, h, away=-1):
        return chip_at(place + away * t * step) * 2 + (core + h) % 2

    cut = rows // SPLIT

    def ring(t, h, i):
        k = piece(t, h)
        at, index = pl.ds(i * cut, cut), (2 * t + h) * SPLIT + i
        return remote(picked.at[k, at], picked.at[k, at], ring_send.at[index], ring_recv.at[index], following)

    def pair(t, h, i):
        k = piece(t, h)
        at, index = pl.ds(i * cut, cut), (2 * t + h) * SPLIT + i
        return remote(picked.at[k, at], picked.at[k, at], pair_send.at[index], pair_recv.at[index], sibling)

    def use_base(k):
        total[...] += dot(picked[k], weight[columns(k), :])

    def use_code(k):
        code_acc[...] += dot(factor_a[:, columns(k)], picked[k], ((1,), (1,)))

    def use(k):
        use_base(k)
        use_code(k)

    for i in range(SPLIT):
        pair(0, 0, i).start()
        ring(0, 0, i).start()
    total[...] = jnp.zeros_like(total)
    code_acc[...] = jnp.zeros_like(code_acc)
    for i in range(SPLIT):
        pair(0, 0, i).wait_recv()
        ring(0, 1, i).start()
    back_half.wait()
    for c in range(chips):
        back_out[c, core] = back_out[c, core] + back_pair[c]
    back_in[chip] = back_out[chip, core]
    each_chip(lambda offset: back_copy(offset).start())
    load_a.wait()
    for copy in load_w:
        copy.wait()
    use(me)

    def forward(t, h):
        for i in range(SPLIT):
            ring(t - 1, h, i).wait_recv()
            pair(t, h, i).start()
            if h == 0:
                ring(t, 0, i).start()
            else:
                @pl.when(t < half - 1)
                def _():
                    ring(t, 1, i).start()

    def hop(t, carry):
        forward(t, 0)
        use(jnp.where(t == 1, sibling, piece(t - 1, 1)))
        forward(t, 1)
        use(piece(t, 0))

        @pl.when(t > 1)
        def _():
            for h in range(2):
                for i in range(SPLIT):
                    pair(t - 1, h, i).wait_recv()
                use(piece(t - 1, 1 - h, 1))
        return carry

    lax.fori_loop(1, half, hop, 0)
    for i in range(SPLIT):
        ring(half - 1, 0, i).wait_recv()
        pair(half, 0, i).start()
    late = [sibling if half == 1 else piece(half - 1, 1), piece(half, 0)]
    for k in late:
        use_code(k)
    if half > 1:
        for h in range(2):
            for i in range(SPLIT):
                pair(half - 1, h, i).wait_recv()
            late.append(piece(half - 1, 1 - h, 1))
            use_code(late[-1])
    use_base(late[0])
    for i in range(SPLIT):
        pair(half, 0, i).wait_recv()
    late.append(piece(half, 1, 1))
    use_code(late[-1])

    codes[me] = code_acc[...].astype(jnp.bfloat16)

    def code_copy(offset):
        k = (me + offset) % n
        return remote(codes.at[me], codes.at[me], code_send.at[offset], code_recv.at[offset], k)

    each(lambda offset: code_copy(offset).start())

    for k in late[1:]:
        use_base(k)
    store_total = local(total, total_out, 0)
    store_total.start()
    each_chip(lambda offset: back_copy(offset).wait_recv())
    back_sum = jnp.sum(back_in[...], axis=0)
    back_b = jnp.where(slot_of[:1] == me, back_sum, 0.0).astype(jnp.bfloat16)
    for k in range(n):
        grad_a[:, k * chunk:(k + 1) * chunk] = SCALE * dot(back_b, picked[k])
    store_a = local(grad_a, grad_a_out, 1)
    store_a.start()

    adapter_of = lax.broadcasted_iota(jnp.int32, (n * rank, rows), 0) // rank
    each(lambda offset: code_copy(offset).wait_recv())
    code_rows = codes[...].astype(jnp.float32).reshape(n * rank, rows)
    code_b[...] = jnp.where(slot_of[:1] == adapter_of, code_rows, 0.0).astype(jnp.bfloat16)
    store_codes = local(code_b, codes_out, 2)
    store_codes.start()

    each(lambda offset: stage_copy(offset).wait_send())
    each(lambda offset: code_copy(offset).wait_send())
    each_chip(lambda offset: back_copy(offset).wait_send())

    def ended(t, carry):
        for i in range(SPLIT):
            ring(t, 0, i).wait_send()
            pair(t, 0, i).wait_send()
        return carry

    def ended_other(t, carry):
        for i in range(SPLIT):
            ring(t - 1, 1, i).wait_send()
            pair(t, 1, i).wait_send()
        return carry

    lax.fori_loop(0, half, ended, 0)
    for i in range(SPLIT):
        pair(half, 0, i).wait_send()
    lax.fori_loop(1, half, ended_other, 0)
    for copy in (store_total, store_a, store_codes):
        copy.wait()


def finish(total_in, grad_a_in, codes_in, adapter_b, cotangent, mixed_out, grad_a_out, grad_b_out, total, codes,
           factor_b, upstream, grad_a, mixed, grad_b, sem):
    def local(src, dst, index):
        return pltpu.make_async_copy(src, dst, sem.at[index])

    loads = [local(codes_in, codes, 0), local(cotangent, upstream, 1), local(adapter_b, factor_b, 2),
             local(total_in, total, 3), local(grad_a_in, grad_a, 4)]
    for copy in loads:
        copy.start()
    stores = []
    loads[0].wait()
    loads[1].wait()
    share = grad_b.shape[0] // OUT_PARTS
    for i in range(OUT_PARTS):
        at = pl.ds(i * share, share)
        grad_b[at] = SCALE * dot(codes[at], upstream[...])
        stores.append(local(grad_b.at[at], grad_b_out.at[at], 7 + i))
        stores[-1].start()
    loads[4].wait()
    stores.append(local(grad_a, grad_a_out, 5))
    stores[-1].start()
    loads[2].wait()
    loads[3].wait()
    code_rows = codes[...].astype(jnp.float32).T.astype(jnp.bfloat16)
    mixed[...] = (total[...] + SCALE * dot(code_rows, factor_b[...])).astype(jnp.bfloat16)
    stores.append(local(mixed, mixed_out, 6))
    stores[-1].start()
    for copy in stores:
        copy.wait()


def on_device(rows_y, tokens, block_job, source, adapter_home, up_weight, adapter_a, adapter_b, cotangent):
    n = lax.axis_size("dp")
    width = tokens.shape[1]
    rows, hidden = cotangent.shape
    jobs, rank, _ = adapter_b.shape
    chunk = width // n
    factor_b = adapter_b.reshape(jobs * rank, hidden)
    smem = pl.BlockSpec(memory_space=pltpu.SMEM)
    anywhere = pl.BlockSpec(memory_space=pl.ANY)
    bf16, f32 = jnp.bfloat16, jnp.float32
    dma = lambda count: pltpu.SemaphoreType.DMA((count,))
    base, grad_a, codes = pl.pallas_call(
        functools.partial(kernel, n, rows_y, rank),
        out_shape=(
            jax.ShapeDtypeStruct((rows, hidden), f32),
            jax.ShapeDtypeStruct((rank, width), f32),
            jax.ShapeDtypeStruct((jobs * rank, rows), bf16),
        ),
        in_specs=[smem] * 3 + [anywhere] * 5,
        out_specs=(anywhere,) * 3,
        scratch_shapes=[
            pltpu.VMEM((width, hidden), bf16),
            pltpu.VMEM((rank, width), bf16),
            pltpu.VMEM((jobs * rank, hidden), bf16),
            pltpu.VMEM((rows, hidden), bf16),
            pltpu.VMEM((n,) + (tokens.shape[0], chunk), bf16),
            pltpu.VMEM((n, rows, chunk), bf16),
            pltpu.VMEM((rows, hidden), f32),
            pltpu.VMEM((rank, rows), f32),
            pltpu.VMEM((rank, width), f32),
            pltpu.VMEM((jobs * rank, rows), bf16),
            pltpu.VMEM((n // 2, 2, rank, rows), f32),
            pltpu.VMEM((n // 2, rank, rows), f32),
            pltpu.VMEM((n // 2, rank, rows), f32),
            pltpu.VMEM((n, rank, rows), bf16),
            dma(4 + W_PARTS),
        ] + [dma(n)] * 2 + [dma(n // 2)] * 2 + [dma(n)] * 2 + [dma(n * SPLIT)] * 2 + [dma((n // 2 + 1) * SPLIT)] * 2,
        compiler_params=pltpu.CompilerParams(
            collective_id=0, has_side_effects=True, vmem_limit_bytes=60 * 1024 * 1024
        ),
    )(
        source, block_job, adapter_home, tokens, up_weight, adapter_a[0].T,
        factor_b, cotangent,
    )
    mixed, grad_a, grad_b = pl.pallas_call(
        finish,
        out_shape=(
            jax.ShapeDtypeStruct((rows, hidden), bf16),
            jax.ShapeDtypeStruct((rank, width), f32),
            jax.ShapeDtypeStruct((jobs * rank, hidden), f32),
        ),
        in_specs=[anywhere] * 5,
        out_specs=(anywhere,) * 3,
        scratch_shapes=[
            pltpu.VMEM((rows, hidden), f32),
            pltpu.VMEM((jobs * rank, rows), bf16),
            pltpu.VMEM((jobs * rank, hidden), bf16),
            pltpu.VMEM((rows, hidden), bf16),
            pltpu.VMEM((rank, width), f32),
            pltpu.VMEM((rows, hidden), bf16),
            pltpu.VMEM((jobs * rank, hidden), f32),
            dma(7 + OUT_PARTS),
        ],
        compiler_params=pltpu.CompilerParams(vmem_limit_bytes=60 * 1024 * 1024),
    )(base, grad_a, codes, factor_b, cotangent)
    return mixed, grad_a.T[None], grad_b.reshape(jobs, rank, hidden)


def solution(mesh):
    placed = (
        P(("groups", "dp"), None),
        P("groups"),
        P("groups"),
        P("groups"),
        P(None, "dp"),
        P(("groups", "dp"), None, None),
        P("groups", None, "dp"),
        P("groups", "dp"),
    )
    rows_y = 2 if mesh.shape["groups"] == 2 else 1
    return jax.shard_map(
        functools.partial(on_device, rows_y),
        mesh=mesh,
        in_specs=placed,
        out_specs=(P("groups", "dp"), P(("groups", "dp"), None, None), P("groups", None, "dp")),
        check_vma=False,
    )
```
